256 devices in a mesh: leaf: 64 (over y, z, core), slab: 4 (over x).
Axes of the slice: x: 4, y: 4, z: 8, core: 2. Of those that a mesh axis runs over, the one named last changes fastest.
Arguments:
- rhs: bfloat16 [8, 1048576], P(None, ('leaf', 'slab')), may hold values from -6 to 6
- col_basis: bfloat16 [4096, 64, 256], P(('leaf', 'slab')), may hold values from -0.375 to 0.375
- row_basis: bfloat16 [4096, 64, 256], P(('leaf', 'slab')), may hold values from -0.75 to 0.75
- near_blocks: bfloat16 [4096, 3, 256, 256], P(('leaf', 'slab')), may hold values from -0.21875 to 0.21875
- near_partner: int32 [4096, 3], P(('leaf', 'slab')), may hold values from 0 to 4095, as said below
- near_count: int32 [4096], P(('leaf', 'slab')), may hold values from 2 to 3
- col_transfer_local: float32 [7680, 64, 64], P(('leaf', 'slab')), may hold values from -0.5 to 0.5
- row_transfer_local: float32 [7680, 64, 64], P(('leaf', 'slab')), may hold values from -0.75 to 0.75
- local_coupling: float32 [7168, 4, 64, 64], P(('leaf', 'slab')), may hold values from -0.375 to 0.375
- local_partner: int32 [7168, 4], P(('leaf', 'slab')), may hold values from 0 to 4095, as said below
- local_count: int32 [7168], P(('leaf', 'slab')), may hold values from 0 to 4, as said below
- col_transfer_up: float32 [256, 6, 64, 64], P(('leaf', 'slab')), as said below
- row_transfer_up: float32 [256, 6, 64, 64], P(('leaf', 'slab')), as said below
- up_coupling: float32 [256, 7, 4, 64, 64], P(('leaf', 'slab')), as said below
- up_partner: int32 [256, 7, 4], P(('leaf', 'slab')), may hold values from 0 to 255, as said below
- up_count: int32 [256, 7], P(('leaf', 'slab')), may hold values from 0 to 4, as said below
Outputs:
- result: float32 [8, 1048576], P(None, ('leaf', 'slab'))
The draws below stay inside these ranges and needn't reach their ends.
Inputs may be any that keep to these rules, and one draw needn't show every extreme that they name: `near_partner`: slot 0 of leaf i holds i. Slot 1 holds a leaf 1 or 2 places above i when i mod 16 >= 8, and 1 or 2 places below i otherwise. Slot 2 holds a leaf 1 or 2 places on the other side. Where a side has no such leaf (the ends of the range), leaves 1 and 2 places on the existing side are used. All three slots are distinct. `local_partner`: entries of level h (h < log2 16 - 1), ordered as crow in the reference program, are clusters of that level; the first local_count slots of cluster j hold distinct clusters 2 or 3 places from j, the remaining slots hold j. `local_count`: at most the number of clusters 2 or 3 places from the cluster that exist. `up_partner`: entry [d, u] describes the ancestor j = d div 2^u of device d at level log2 16 + u and is the same for all devices with that ancestor; its first up_count slots hold distinct clusters 2 or 3 places from j, the remaining slots hold j. `up_count`: same for all devices with a common ancestor at that level; at most the number of clusters 2 or 3 places away that exist. `col_transfer_up`: entry [d, u] is the same for all devices with a common ancestor at level log2 16 + u. `row_transfer_up`: entry [d, u] is the same for all devices with a common ancestor at level log2 16 + u. `up_coupling`: entry [d, u] is the same for all devices with a common ancestor at level log2 16 + u.
All inputs are finite; a program needn't handle non-finite values.
Results may differ from the reference program's by a relative error of at most 0.0029.
Values may be sent and summed in bfloat16 or wider, within the bound.
No kernel may reach another device: no remote copies, remote signals or barrier semaphores. Data moves between devices by JAX's collectives and lax.ppermute only.
A program may use at most 64 MiB of HBM per device.

```python
import jax
import jax.numpy as jnp
from jax import lax

LEAF = 256
K = 64
R = 8
LD = 16
NP = 3
CP = 4
NDEV = 256
UPL = 8
NL = 4096
NPTS = 1048576
LT = 30
LC = 28


def pick_counted(key, total):
    first, second = jax.random.split(key)
    offsets = jnp.array([-3, -2, 2, 3], jnp.int32)
    own = jnp.arange(total, dtype=jnp.int32)[:, None]
    spots = own + offsets[None, :]
    wrong = ((spots < 0) | (spots >= total)).astype(jnp.int32)
    score = wrong * 16 + jax.random.randint(first, (total, 4), 0, 4) * 4 + jnp.arange(4, dtype=jnp.int32)[None, :]
    order = jnp.argsort(score, axis=1)
    spots = jnp.take_along_axis(spots, order, axis=1)
    wrong = jnp.take_along_axis(wrong, order, axis=1)
    count = jnp.maximum(4 - wrong.sum(axis=1) - jax.random.randint(second, (total,), 0, 2), 0).astype(jnp.int32)
    used = jnp.arange(4, dtype=jnp.int32)[None, :] < count[:, None]
    return (jnp.where(used, spots, own).astype(jnp.int32), count)


def local_lists(key):
    depth = LD.bit_length() - 1
    partners = []
    counts = []
    for level in range(depth - 1):
        width = LD >> level
        spots, count = pick_counted(jax.random.fold_in(key, level), NL >> level)
        partners.append(spots.reshape(NDEV, width, CP))
        counts.append(count.reshape(NDEV, width))
    return (jnp.concatenate(partners, axis=1).reshape(NDEV * LC, CP), jnp.concatenate(counts, axis=1).reshape(NDEV * LC))


def upper_lists(key):
    partners = []
    counts = []
    for tier in range(UPL - 1):
        spots, count = pick_counted(jax.random.fold_in(key, tier), NDEV >> tier)
        partners.append(jnp.repeat(spots, 1 << tier, axis=0))
        counts.append(jnp.repeat(count, 1 << tier, axis=0))
    return (jnp.stack(partners, axis=1), jnp.stack(counts, axis=1))


def node_values(key, tiers, tail, scale):
    pieces = []
    for tier in range(tiers):
        drawn = jax.random.normal(jax.random.fold_in(key, tier), (NDEV >> tier,) + tail, jnp.float32) * scale
        pieces.append(jnp.repeat(drawn, 1 << tier, axis=0))
    return jnp.stack(pieces, axis=1)


def draw_near_partner(key, part):
    key = jax.random.fold_in(key, 13)
    first, second = jax.random.split(key)
    own = jnp.arange(NL, dtype=jnp.int32)
    upper_half = own % LD >= LD // 2
    up_spot = own + jax.random.randint(first, (NL,), 1, 3)
    up_spot = jnp.where(up_spot >= NL, own + 1, up_spot)
    down_spot = own - jax.random.randint(second, (NL,), 1, 3)
    down_spot = jnp.where(down_spot < 0, own - 1, down_spot)
    main_spot = jnp.where(upper_half, up_spot, down_spot)
    other_spot = jnp.where(upper_half, down_spot, up_spot)
    at_top = own == NL - 1
    at_bottom = own == 0
    main_spot = jnp.where(at_top, own - 1, jnp.where(at_bottom, own + 1, main_spot))
    other_spot = jnp.where(at_top, own - 2, jnp.where(at_bottom, own + 2, other_spot))
    return jnp.stack([own, main_spot, other_spot], axis=1).astype(jnp.int32)


def draw_local_partner(key, part):
    return local_lists(jax.random.fold_in(key, 21))[0]


def draw_local_count(key, part):
    return local_lists(jax.random.fold_in(key, 21))[1]


def draw_up_partner(key, part):
    return upper_lists(jax.random.fold_in(key, 31))[0]


def draw_up_count(key, part):
    return upper_lists(jax.random.fold_in(key, 31))[1]


def draw_col_transfer_up(key, part):
    key = jax.random.fold_in(key, 3)
    return node_values(key, UPL - 2, (K, K), (2.0 * K) ** (-0.5))


def draw_row_transfer_up(key, part):
    key = jax.random.fold_in(key, 5)
    return node_values(key, UPL - 2, (K, K), (1.0 * K) ** (-0.5))


def draw_up_coupling(key, part):
    key = jax.random.fold_in(key, 7)
    return node_values(key, UPL - 1, (CP, K, K), (1.0 * K * CP) ** (-0.5))


def touch_ends(result, own_key, least, largest):
    longest = result.shape.index(max(result.shape))
    spots = []
    for shift in (0, 1):
        where = [jax.random.randint(jax.random.fold_in(own_key, axis), (), 0, length) for axis, length in enumerate(result.shape)]
        where[longest] = (where[longest] + shift) % result.shape[longest]
        spots.append(tuple(where))
    return result.at[spots[0]].set(least).at[spots[1]].set(largest)


def block_scale(rng, extent, shards, low, top_value):
    factor_of, own = 1.0, jax.random.fold_in(rng, 6)
    for dim, parts in shards:
        heights = jnp.exp(jax.random.uniform(jax.random.fold_in(own, dim), (parts,), jnp.float32, low / len(shards), top_value / len(shards)))
        factor_of = factor_of * jnp.repeat(heights, extent[dim] // parts).reshape([-1 if axis == dim else 1 for axis in range(len(extent))])
    return factor_of


def centred(key, dims, scale, bound, cuts=(), kind=jnp.bfloat16):
    loudness = block_scale(key, dims, cuts, -0.22, 0.18) if cuts else 1.0
    entries = jax.random.normal(key, dims, jnp.float32) * scale * loudness
    return jnp.minimum(jnp.maximum(entries, -bound), bound).astype(kind)


def setup_inputs(seed: int = 0) -> dict:
    key_of = jax.random.split(jax.random.key(seed), 17)
    rhs = centred(key_of[0], (R, NPTS), 1.0, 6.0, ((1, 256),))
    col_basis = centred(key_of[1], (NL, K, LEAF), LEAF ** -0.5, 0.375, ((0, 256),))
    row_basis = centred(key_of[2], (NL, K, LEAF), K ** -0.5, 0.75, ((0, 256),))
    near_blocks = centred(key_of[3], (NL, NP, LEAF, LEAF), (LEAF * NP) ** -0.5, 0.21875, ((0, 256),))
    near_partner = draw_near_partner(jax.random.fold_in(key_of[16], 71), 0)
    near_count = touch_ends(jax.random.randint(key_of[5], (NL,), 2, NP + 1), jax.random.fold_in(key_of[5], 1), 2, NP).astype(jnp.int32)
    col_transfer_local = centred(key_of[6], (NDEV * LT, K, K), (2 * K) ** -0.5, 0.5, ((0, 256),), jnp.float32)
    row_transfer_local = centred(key_of[7], (NDEV * LT, K, K), K ** -0.5, 0.75, ((0, 256),), jnp.float32)
    local_coupling = centred(key_of[8], (NDEV * LC, CP, K, K), (K * CP) ** -0.5, 0.375, ((0, 256),), jnp.float32)
    local_partner = draw_local_partner(jax.random.fold_in(key_of[16], 71), 0)
    local_count = draw_local_count(jax.random.fold_in(key_of[16], 71), 0)
    col_transfer_up = draw_col_transfer_up(jax.random.fold_in(key_of[16], 71), 0)
    row_transfer_up = draw_row_transfer_up(jax.random.fold_in(key_of[16], 71), 0)
    up_coupling = draw_up_coupling(jax.random.fold_in(key_of[16], 71), 0)
    up_partner = draw_up_partner(jax.random.fold_in(key_of[16], 71), 0)
    up_count = draw_up_count(jax.random.fold_in(key_of[16], 71), 0)
    return dict(rhs=rhs, col_basis=col_basis, row_basis=row_basis, near_blocks=near_blocks, near_partner=near_partner, near_count=near_count, col_transfer_local=col_transfer_local, row_transfer_local=row_transfer_local, local_coupling=local_coupling, local_partner=local_partner, local_count=local_count, col_transfer_up=col_transfer_up, row_transfer_up=row_transfer_up, up_coupling=up_coupling, up_partner=up_partner, up_count=up_count)


def local_rows(array, per, level):
    start = sum(LD >> g for g in range(level))
    width = LD >> level
    shaped = array.reshape((NDEV, per) + array.shape[1:])
    return shaped[:, start:start + width].reshape((NDEV * width,) + array.shape[1:])


def couple(coeffs, partner, count, coupling):
    live = (jnp.arange(CP)[None, :] < count[:, None]).astype(jnp.float32)
    chosen = coeffs[partner] * live[:, :, None, None]
    return jnp.einsum("isrk,iskj->irj", chosen, coupling, precision=lax.Precision.HIGHEST)


def reference(rhs, col_basis, row_basis, near_blocks, near_partner, near_count, col_transfer_local, row_transfer_local, local_coupling, local_partner, local_count, col_transfer_up, row_transfer_up, up_coupling, up_partner, up_count):
    highest = lax.Precision.HIGHEST
    depth = LD.bit_length() - 1
    tiers = UPL - 1
    points = rhs.reshape(R, NL, LEAF)
    up = [jnp.einsum("rlp,lkp->lrk", points.astype(jnp.float32), col_basis.astype(jnp.float32), precision=highest)]
    for level in range(depth + tiers - 1):
        if level < depth:
            trans = local_rows(col_transfer_local, LT, level)
        else:
            tier = level - depth
            trans = col_transfer_up[::1 << tier, tier]
        moved = jnp.einsum("irk,ikj->irj", up[-1], trans, precision=highest)
        up.append(moved.reshape(-1, 2, R, K).sum(axis=1))
    far = {}
    for level in range(depth - 1):
        far[level] = couple(up[level], local_rows(local_partner, LC, level), local_rows(local_count, LC, level), local_rows(local_coupling, LC, level))
    for tier in range(tiers):
        step = 1 << tier
        far[depth + tier] = couple(up[depth + tier], up_partner[::step, tier], up_count[::step, tier], up_coupling[::step, tier])
    top = depth + tiers - 1
    field = far[top]
    for level in range(top - 1, -1, -1):
        if level < depth:
            trans = local_rows(row_transfer_local, LT, level)
        else:
            tier = level - depth
            trans = row_transfer_up[::1 << tier, tier]
        moved = jnp.einsum("irk,ikj->irj", jnp.repeat(field, 2, axis=0), trans, precision=highest)
        if level in far:
            field = far[level] + moved
        else:
            field = moved
    leaf_field = field.astype(jnp.bfloat16)
    far_out = jnp.einsum("lrk,lkp->rlp", leaf_field.astype(jnp.float32), row_basis.astype(jnp.float32), precision=highest)
    live = jnp.arange(NP)[None, :] < near_count[:, None]
    taken = jnp.where(live[None, :, :, None], points[:, near_partner], jnp.zeros((), jnp.bfloat16))
    taken = taken.reshape(R, NDEV, LD, NP, LEAF).transpose(1, 0, 2, 3, 4)
    blocks = near_blocks.reshape(NDEV, LD, NP, LEAF, LEAF)

    def near_device(pair):
        return jnp.einsum("lspq,rlsq->rlp", pair[0].astype(jnp.float32), pair[1].astype(jnp.float32), precision=highest)

    near = lax.map(near_device, (blocks, taken))
    near = near.transpose(1, 0, 2, 3).reshape(R, NL, LEAF)
    return (near + far_out).reshape(R, NPTS)
```

```python
import jax
import jax.numpy as jnp
from jax import lax
from jax.experimental import pallas as pl
from jax.experimental.pallas import tpu as pltpu
from jax.sharding import PartitionSpec as P

AXES = ("leaf", "slab")
F32 = jnp.float32
BF16 = jnp.bfloat16
LEAVES = 16
LEAF_LEN = 256
RANK = 64
NRHS = 8
TIERS = 7
SLOTS = 4
NDEV = 256
STARTS = (0, 16, 24, 28)
ROWS = (0, 16, 24)
EDGE = 2 * LEAF_LEN
HALO = EDGE + 10 * RANK
ZERO = 6


def mxu(left, right):
    return lax.dot_general(left, right, (((1,), (0,)), ((), ())), preferred_element_type=F32)


def mxu_t(left, right):
    return lax.dot_general(left, right, (((1,), (1,)), ((), ())), preferred_element_type=F32)


def split(value):
    high = value.astype(BF16)
    return high, (value - high.astype(F32)).astype(BF16)


def stacked(value):
    high = value.astype(BF16).astype(F32)
    return jnp.concatenate([high, value - high], axis=0).astype(BF16)


def folded(left, high, low):
    total = mxu(left, high) + mxu(left, low)
    half = total.shape[0] // 2
    return total[:half] + total[half:]


def product(left, right):
    return folded(stacked(left), *split(right))


def up_kernel(rhs, col_basis, col_local, col_up, blocks, coeffs, halo_up, halo_down):
    me = lax.axis_index("leaf") * 4 + lax.axis_index("slab")
    blocks[...] = jnp.zeros_like(blocks)
    level = [
        mxu_t(rhs[:, l * LEAF_LEN : (l + 1) * LEAF_LEN], col_basis[l]) for l in range(LEAVES)
    ]
    spot = 0
    for h in range(4):
        width = LEAVES >> h
        if h < 3:
            for c in range(width):
                coeffs[ROWS[h] + c] = level[c]
            for i in range(3):
                at = EDGE + (h * 3 + i) * RANK
                halo_up[:, at : at + RANK] = level[width - 3 + i].astype(BF16)
                halo_down[:, at : at + RANK] = level[i].astype(BF16)
        above = []
        for j in range(width // 2):
            pair = jnp.concatenate([level[2 * j], level[2 * j + 1]], axis=1)
            moves = col_local[STARTS[h] + 2 * j : STARTS[h] + 2 * j + 2].reshape(2 * RANK, RANK)
            above.append(product(pair, moves))
        level = above
    halo_up[:, :EDGE] = rhs[:, (LEAVES - 2) * LEAF_LEN :]
    halo_down[:, :EDGE] = rhs[:, :EDGE]
    halo_up[:, HALO - RANK :] = jnp.zeros((NRHS, RANK), BF16)
    halo_down[:, HALO - RANK :] = jnp.zeros((NRHS, RANK), BF16)
    share = level[0]
    for u in range(TIERS):
        sent = share.astype(BF16)
        side = (u % 2) * RANK
        span = 1 << u
        own = lax.shift_right_logical(me, u)
        for off in (-3, -2, 2, 3):
            there = own + off

            @pl.when((there >= 0) & (there < (NDEV >> u)))
            def _():
                blocks[pl.ds(there * span, span), :, side : side + RANK] = jnp.broadcast_to(
                    sent[None], (span, NRHS, RANK)
                )

        if u < TIERS - 1:
            share = product(share, col_up[0, u])


def near_leaf(l, me, window, shift, blocks, partner, count):
    total = None
    for s in range(3):
        spot = partner[l, s] - me * LEAVES + shift
        part = window[:, pl.ds(pl.multiple_of(spot * LEAF_LEN, LEAF_LEN), LEAF_LEN)]
        if s == 2:
            part = jnp.where(count[l] > s, part, jnp.zeros_like(part))
        term = mxu_t(part, blocks[s])
        total = term if total is None else total + term
    return total


def inner_kernel(
    rhs, near_blocks, partner, count, row_local, row_up, coupling, near, paths, pairs, held, sems
):
    me = lax.axis_index("leaf") * 4 + lax.axis_index("slab")
    inner = LEAVES - 4
    copies = [
        pltpu.make_async_copy(near_blocks.at[2 + l], held.at[l], sems.at[l]) for l in range(inner)
    ]
    for copy in copies:
        copy.start()
    level = [row_local[STARTS[3] + c] for c in range(2)]
    for h in (2, 1, 0):
        level = [
            product(level[c // 2], row_local[STARTS[h] + c]) for c in range(LEAVES >> h)
        ]
    for l in range(LEAVES):
        high, low = split(level[l])
        paths[0, :, l * RANK : (l + 1) * RANK] = high
        paths[1, :, l * RANK : (l + 1) * RANK] = low
    for u in range(TIERS):
        high, low = split(coupling[0, u].reshape(SLOTS * RANK, RANK))
        pairs[0, u * 256 : (u + 1) * 256] = high
        pairs[1, u * 256 : (u + 1) * 256] = low
    for u in range(TIERS - 1):
        high, low = split(row_up[0, u])
        at = TIERS * 256 + u * RANK
        pairs[0, at : at + RANK] = high
        pairs[1, at : at + RANK] = low
    for l in range(inner):
        copies[l].wait()
        near[:, l * LEAF_LEN : (l + 1) * LEAF_LEN] = near_leaf(
            l + 2, me, rhs, 0, held.at[l], partner, count
        )


def edge_kernel(
    rhs,
    from_low,
    from_high,
    coeffs,
    near_blocks,
    partner,
    count,
    coupling,
    local_partner,
    local_count,
    row_local,
    near,
    field,
    held,
    sems,
    window,
    left,
    right,
):
    me = lax.axis_index("leaf") * 4 + lax.axis_index("slab")
    leaves = (0, 1, LEAVES - 2, LEAVES - 1)
    copies = [
        pltpu.make_async_copy(near_blocks.at[l], held.at[i], sems.at[i])
        for i, l in enumerate(leaves)
    ]
    for copy in copies:
        copy.start()
    window[:, :EDGE] = from_low[:, :EDGE]
    window[:, EDGE : EDGE + LEAVES * LEAF_LEN] = rhs[...]
    window[:, EDGE + LEAVES * LEAF_LEN :] = from_high[:, :EDGE]
    blank = jnp.zeros((2 * NRHS, RANK), F32)

    def place(at, value):
        high = value.astype(BF16).astype(F32)
        both = jnp.concatenate([high, value - high], axis=0)
        left[at] = jnp.concatenate([both, blank], axis=1)
        right[at] = jnp.concatenate([blank, both], axis=1)

    far = []
    base = 0
    for h in range(3):
        width = LEAVES >> h
        for i in range(3):
            at = EDGE + (h * 3 + i) * RANK
            place(base + i, from_low[:, at : at + RANK].astype(F32))
            place(base + 3 + width + i, from_high[:, at : at + RANK].astype(F32))
        for c in range(width):
            place(base + 3 + c, coeffs[ROWS[h] + c])
        none = base + width + ZERO
        left[none] = jnp.zeros((2 * NRHS, 2 * RANK), F32)
        right[none] = jnp.zeros((2 * NRHS, 2 * RANK), F32)
        terms = []
        for c in range(width):
            row = ROWS[h] + c
            live = local_count[row]
            spots = [
                jnp.where(s < live, local_partner[row, s] - me * width + (base + 3), none)
                for s in range(SLOTS)
            ]
            chosen = jnp.concatenate(
                [left[spots[0]] + right[spots[1]], left[spots[2]] + right[spots[3]]], axis=1
            ).astype(BF16)
            terms.append(folded(chosen, *split(coupling[row].reshape(SLOTS * RANK, RANK))))
        far.append(terms)
        base += width + ZERO + 1
    level = far[2]
    for h in (1, 0):
        level = [
            far[h][c] + product(level[c // 2], row_local[STARTS[h] + c])
            for c in range(LEAVES >> h)
        ]
    for l in range(LEAVES):
        field[:, l * RANK : (l + 1) * RANK] = level[l]
    for i, l in enumerate(leaves):
        copies[i].wait()
        near[:, i * LEAF_LEN : (i + 1) * LEAF_LEN] = near_leaf(
            l, me, window, 2, held.at[i], partner, count
        )


def final_kernel(
    got, partner, count, pairs, paths, field, near_inner, near_edge, row_basis, out
):
    lane = lax.broadcasted_iota(jnp.int32, (NRHS, 2 * RANK), 1)
    far = []
    for u in range(TIERS):
        span = 1 << u
        live = count[0, u]
        sums = []
        for s in range(SLOTS):
            block = got[pl.ds(partner[0, u, s] * span, span)].astype(F32)
            total = jnp.where(s < live, jnp.sum(block, axis=0), 0.0)
            sums.append(total if s % 2 == u % 2 else pltpu.roll(total, RANK, 1))
        chosen = jnp.concatenate(
            [
                jnp.where(lane < RANK, sums[0], sums[1]),
                jnp.where(lane < RANK, sums[2], sums[3]),
            ],
            axis=1,
        )
        rows = slice(u * 256, (u + 1) * 256)
        far.append(folded(stacked(chosen), pairs[0, rows], pairs[1, rows]))
    down = far[TIERS - 1]
    for u in reversed(range(TIERS - 1)):
        at = TIERS * 256 + u * RANK
        rows = slice(at, at + RANK)
        down = far[u] + folded(stacked(down), pairs[0, rows], pairs[1, rows])
    leaf_field = field[...] + folded(stacked(down), paths[0], paths[1])
    both = stacked(leaf_field)
    for l in range(LEAVES):
        total = mxu(both[:, l * RANK : (l + 1) * RANK], row_basis[l])
        if 2 <= l < LEAVES - 2:
            near = near_inner[:, (l - 2) * LEAF_LEN : (l - 1) * LEAF_LEN]
        else:
            i = l if l < 2 else l - (LEAVES - 4)
            near = near_edge[:, i * LEAF_LEN : (i + 1) * LEAF_LEN]
        out[:, l * LEAF_LEN : (l + 1) * LEAF_LEN] = near + total[:NRHS] + total[NRHS:]


VMEM = pl.BlockSpec(memory_space=pltpu.VMEM)
SMEM = pl.BlockSpec(memory_space=pltpu.SMEM)
ANY = pl.BlockSpec(memory_space=pl.ANY)
LIMIT = pltpu.CompilerParams(vmem_limit_bytes=24 * 1024 * 1024)


def cost(flops, size):
    return pl.CostEstimate(flops=flops, bytes_accessed=size, transcendentals=0)


def body(
    rhs,
    col_basis,
    row_basis,
    near_blocks,
    near_partner,
    near_count,
    col_transfer_local,
    row_transfer_local,
    local_coupling,
    local_partner,
    local_count,
    col_transfer_up,
    row_transfer_up,
    up_coupling,
    up_partner,
    up_count,
):
    shape = jax.ShapeDtypeStruct
    blocks, coeffs, halo_up, halo_down = pl.pallas_call(
        up_kernel,
        out_shape=(
            shape((NDEV, NRHS, 2 * RANK), BF16),
            shape((28, NRHS, RANK), F32),
            shape((NRHS, HALO), BF16),
            shape((NRHS, HALO), BF16),
        ),
        in_specs=[VMEM] * 4,
        out_specs=(VMEM,) * 4,
        compiler_params=LIMIT,
        cost_estimate=cost(2 * 10**7, 4 * 10**6),
    )(rhs, col_basis, col_transfer_local, col_transfer_up)
    ups = [(i, i + 1) for i in range(NDEV - 1)]
    downs = [(i + 1, i) for i in range(NDEV - 1)]
    got = lax.all_to_all(blocks, AXES, 0, 0)
    from_low = lax.ppermute(halo_up, AXES, ups)
    from_high = lax.ppermute(halo_down, AXES, downs)
    inner = LEAVES - 4
    near_inner, paths, pairs = pl.pallas_call(
        inner_kernel,
        out_shape=(
            shape((NRHS, inner * LEAF_LEN), F32),
            shape((2, RANK, LEAVES * RANK), BF16),
            shape((2, TIERS * 256 + (TIERS - 1) * RANK, RANK), BF16),
        ),
        in_specs=[VMEM, ANY, SMEM, SMEM, VMEM, VMEM, VMEM],
        out_specs=(VMEM,) * 3,
        scratch_shapes=[
            pltpu.VMEM((inner, 3, LEAF_LEN, LEAF_LEN), BF16),
            pltpu.SemaphoreType.DMA((inner,)),
        ],
        compiler_params=LIMIT,
        cost_estimate=cost(2 * 10**8, 10**7),
    )(
        rhs,
        near_blocks,
        near_partner,
        near_count,
        row_transfer_local,
        row_transfer_up,
        up_coupling,
    )
    entries = 28 + 3 * (ZERO + 1)
    near_edge, field = pl.pallas_call(
        edge_kernel,
        out_shape=(shape((NRHS, 4 * LEAF_LEN), F32), shape((NRHS, LEAVES * RANK), F32)),
        in_specs=[VMEM, VMEM, VMEM, VMEM, ANY, SMEM, SMEM, VMEM, SMEM, SMEM, VMEM],
        out_specs=(VMEM,) * 2,
        scratch_shapes=[
            pltpu.VMEM((4, 3, LEAF_LEN, LEAF_LEN), BF16),
            pltpu.SemaphoreType.DMA((4,)),
            pltpu.VMEM((NRHS, LEAVES * LEAF_LEN + 2 * EDGE), BF16),
            pltpu.VMEM((entries, 2 * NRHS, 2 * RANK), F32),
            pltpu.VMEM((entries, 2 * NRHS, 2 * RANK), F32),
        ],
        compiler_params=LIMIT,
        cost_estimate=cost(10**8, 7 * 10**6),
    )(
        rhs,
        from_low,
        from_high,
        coeffs,
        near_blocks,
        near_partner,
        near_count,
        local_coupling,
        local_partner,
        local_count,
        row_transfer_local,
    )
    return pl.pallas_call(
        final_kernel,
        out_shape=shape((NRHS, LEAVES * LEAF_LEN), F32),
        in_specs=[VMEM, SMEM, SMEM] + [VMEM] * 6,
        out_specs=VMEM,
        compiler_params=LIMIT,
        cost_estimate=cost(2 * 10**7, 3 * 10**6),
    )(got, up_partner, up_count, pairs, paths, field, near_inner, near_edge, row_basis)


def solution(mesh):
    return jax.shard_map(
        body,
        mesh=mesh,
        in_specs=(
            P(None, AXES),
            P(AXES, None, None),
            P(AXES, None, None),
            P(AXES, None, None, None),
            P(AXES, None),
            P(AXES),
            P(AXES, None, None),
            P(AXES, None, None),
            P(AXES, None, None, None),
            P(AXES, None),
            P(AXES),
            P(AXES, None, None, None),
            P(AXES, None, None, None),
            P(AXES, None, None, None, None),
            P(AXES, None, None),
            P(AXES, None),
        ),
        out_specs=P(None, AXES),
        check_vma=False,
    )
```

```python
import jax
import jax.numpy as jnp
from jax import lax
from jax.experimental import pallas as pl
from jax.experimental.pallas import tpu as pltpu
from jax.sharding import PartitionSpec as P

AXES = ("leaf", "slab")
F32 = jnp.float32
BF16 = jnp.bfloat16
LEAVES = 16
LEAF_LEN = 256
RANK = 64
NRHS = 8
TIERS = 7
SLOTS = 4
NDEV = 256
STARTS = (0, 16, 24, 28)
ROWS = (0, 16, 24)
EDGE = 2 * LEAF_LEN
HALO = EDGE + 10 * RANK
ZERO = 6
EARLY = 6


def mxu(left, right):
    return lax.dot_general(left, right, (((1,), (0,)), ((), ())), preferred_element_type=F32)


def mxu_t(left, right):
    return lax.dot_general(left, right, (((1,), (1,)), ((), ())), preferred_element_type=F32)


def split(value):
    high = value.astype(BF16)
    return high, (value - high.astype(F32)).astype(BF16)


def stacked(value):
    high = value.astype(BF16).astype(F32)
    return jnp.concatenate([high, value - high], axis=0).astype(BF16)


def folded(left, high, low):
    total = mxu(left, high) + mxu(left, low)
    half = total.shape[0] // 2
    return total[:half] + total[half:]


def product(left, right):
    return folded(stacked(left), *split(right))


def fetch(sources, targets, sems):
    copies = [
        pltpu.make_async_copy(source, target, sems.at[i])
        for i, (source, target) in enumerate(zip(sources, targets))
    ]
    for copy in copies:
        copy.start()
    return copies


def up_kernel(
    rhs_in,
    basis_in,
    local_in,
    up_in,
    near_in,
    blocks,
    coeffs,
    halo_first,
    halo_second,
    rhs,
    near_blocks,
    col_basis,
    col_local,
    col_up,
    sems,
    halo_up,
    halo_down,
):
    me = lax.axis_index("leaf") * 4 + lax.axis_index("slab")
    copies = fetch(
        (rhs_in, basis_in, local_in, up_in, near_in.at[pl.ds(2, EARLY)]),
        (rhs, col_basis, col_local, col_up, near_blocks),
        sems,
    )
    blocks[...] = jnp.zeros_like(blocks)
    copies[0].wait()
    copies[1].wait()
    level = [
        mxu_t(rhs[:, l * LEAF_LEN : (l + 1) * LEAF_LEN], col_basis[l]) for l in range(LEAVES)
    ]
    copies[2].wait()
    for h in range(4):
        width = LEAVES >> h
        if h < 3:
            for c in range(width):
                coeffs[ROWS[h] + c] = level[c]
            for i in range(3):
                at = EDGE + (h * 3 + i) * RANK
                halo_up[:, at : at + RANK] = level[width - 3 + i].astype(BF16)
                halo_down[:, at : at + RANK] = level[i].astype(BF16)
        above = []
        for j in range(width // 2):
            pair = jnp.concatenate([level[2 * j], level[2 * j + 1]], axis=1)
            moves = col_local[STARTS[h] + 2 * j : STARTS[h] + 2 * j + 2].reshape(2 * RANK, RANK)
            above.append(product(pair, moves))
        level = above
    halo_up[:, :EDGE] = rhs[:, (LEAVES - 2) * LEAF_LEN :]
    halo_down[:, :EDGE] = rhs[:, :EDGE]
    halo_up[:, HALO - RANK :] = jnp.zeros((NRHS, RANK), BF16)
    halo_down[:, HALO - RANK :] = jnp.zeros((NRHS, RANK), BF16)
    even = me % 2 == 0
    halo_first[...] = jnp.where(even, halo_up[...], halo_down[...])
    halo_second[...] = jnp.where(even, halo_down[...], halo_up[...])
    share = level[0]
    copies[3].wait()
    for u in range(TIERS):
        sent = share.astype(BF16)
        side = (u % 2) * RANK
        span = 1 << u
        own = lax.shift_right_logical(me, u)
        for off in (-3, -2, 2, 3):
            there = own + off

            @pl.when((there >= 0) & (there < (NDEV >> u)))
            def _():
                blocks[pl.ds(there * span, span), :, side : side + RANK] = jnp.broadcast_to(
                    sent[None], (span, NRHS, RANK)
                )

        if u < TIERS - 1:
            share = product(share, col_up[0, u])
    copies[4].wait()


def near_leaf(l, me, window, shift, blocks, partner, count):
    total = None
    for s in range(3):
        spot = partner[s, l] - me * LEAVES + shift
        part = window[:, pl.ds(pl.multiple_of(spot * LEAF_LEN, LEAF_LEN), LEAF_LEN)]
        if s == 2:
            part = jnp.where(count[l] > s, part, jnp.zeros_like(part))
        term = mxu_t(part, blocks[s])
        total = term if total is None else total + term
    return total


def inner_kernel(
    rhs,
    near_early,
    near_in,
    partner,
    count,
    coupling_in,
    local_in,
    near,
    paths,
    coupling,
    row_local,
    near_blocks,
    sems,
):
    me = lax.axis_index("leaf") * 4 + lax.axis_index("slab")
    late = LEAVES - 4 - EARLY
    copies = fetch(
        [local_in, coupling_in.at[pl.ds(LEAVES, 12)]]
        + [near_in.at[2 + EARLY + i] for i in range(late)],
        [row_local, coupling] + [near_blocks.at[i] for i in range(late)],
        sems,
    )
    for l in range(2, LEAVES - 2):
        i = l - 2 - EARLY
        if i >= 0:
            copies[2 + i].wait()
        near[:, (l - 2) * LEAF_LEN : (l - 1) * LEAF_LEN] = near_leaf(
            l, me, rhs, 0, near_early.at[l - 2] if i < 0 else near_blocks.at[i], partner, count
        )
    copies[0].wait()
    level = [row_local[STARTS[3] + c] for c in range(2)]
    for h in (2, 1, 0):
        level = [
            product(level[c // 2], row_local[STARTS[h] + c]) for c in range(LEAVES >> h)
        ]
    for l in range(LEAVES):
        high, low = split(level[l])
        paths[0, :, l * RANK : (l + 1) * RANK] = high
        paths[1, :, l * RANK : (l + 1) * RANK] = low
    copies[1].wait()


def edge_kernel(
    rhs,
    first,
    second,
    coeffs,
    near_in,
    partner,
    count,
    coupling_in,
    coupling_held,
    local_partner,
    local_count,
    row_local,
    up_in,
    pairs_in,
    basis_in,
    near,
    field,
    pairs,
    row_basis,
    coupling,
    row_up,
    up_coupling,
    near_blocks,
    sems,
    window,
    left,
    right,
):
    me = lax.axis_index("leaf") * 4 + lax.axis_index("slab")
    edges = (0, 1, LEAVES - 2, LEAVES - 1)
    copies = fetch(
        [coupling_in.at[pl.ds(0, LEAVES)]]
        + [near_in.at[l] for l in edges]
        + [pairs_in, up_in, basis_in],
        [coupling]
        + [near_blocks.at[i] for i in range(4)]
        + [up_coupling, row_up, row_basis],
        sems,
    )
    even = me % 2 == 0
    from_low = jnp.where(even, second[...], first[...])
    from_high = jnp.where(even, first[...], second[...])
    window[:, :EDGE] = from_low[:, :EDGE]
    window[:, EDGE : EDGE + LEAVES * LEAF_LEN] = rhs[...]
    window[:, EDGE + LEAVES * LEAF_LEN :] = from_high[:, :EDGE]
    blank = jnp.zeros((2 * NRHS, RANK), F32)

    def place(at, value):
        high = value.astype(BF16).astype(F32)
        both = jnp.concatenate([high, value - high], axis=0)
        left[at] = jnp.concatenate([both, blank], axis=1)
        right[at] = jnp.concatenate([blank, both], axis=1)

    bases = []
    base = 0
    for h in range(3):
        width = LEAVES >> h
        for i in range(3):
            at = EDGE + (h * 3 + i) * RANK
            place(base + i, from_low[:, at : at + RANK].astype(F32))
            place(base + 3 + width + i, from_high[:, at : at + RANK].astype(F32))
        for c in range(width):
            place(base + 3 + c, coeffs[ROWS[h] + c])
        left[base + width + ZERO] = jnp.zeros((2 * NRHS, 2 * RANK), F32)
        right[base + width + ZERO] = jnp.zeros((2 * NRHS, 2 * RANK), F32)
        bases.append(base)
        base += width + ZERO + 1

    def couple(h, c, matrices):
        row = ROWS[h] + c
        live = local_count[row]
        start = bases[h] + 3 - me * (LEAVES >> h)
        none = bases[h] + (LEAVES >> h) + ZERO
        spots = [
            jnp.where(s < live, local_partner[s, row] + start, none) for s in range(SLOTS)
        ]
        chosen = jnp.concatenate(
            [left[spots[0]] + right[spots[1]], left[spots[2]] + right[spots[3]]], axis=1
        ).astype(BF16)
        return folded(chosen, *split(matrices.reshape(SLOTS * RANK, RANK)))

    level = [couple(2, c, coupling_held[8 + c]) for c in range(4)]
    level = [
        couple(1, c, coupling_held[c]) + product(level[c // 2], row_local[STARTS[1] + c])
        for c in range(8)
    ]
    level = [product(level[c // 2], row_local[c]) for c in range(LEAVES)]
    copies[0].wait()
    for l in range(LEAVES):
        field[:, l * RANK : (l + 1) * RANK] = level[l] + couple(0, l, coupling[l])
    for i, l in enumerate(edges):
        copies[1 + i].wait()
        near[:, i * LEAF_LEN : (i + 1) * LEAF_LEN] = near_leaf(
            l, me, window, 2, near_blocks.at[i], partner, count
        )
    copies[5].wait()
    copies[6].wait()
    for u in range(TIERS):
        high, low = split(up_coupling[0, u].reshape(SLOTS * RANK, RANK))
        pairs[0, u * 256 : (u + 1) * 256] = high
        pairs[1, u * 256 : (u + 1) * 256] = low
    for u in range(TIERS - 1):
        high, low = split(row_up[0, u])
        at = TIERS * 256 + u * RANK
        pairs[0, at : at + RANK] = high
        pairs[1, at : at + RANK] = low
    copies[7].wait()


def final_kernel(
    got, partner, count, pairs, paths, field, near_inner, near_edge, row_basis, out
):
    lane = lax.broadcasted_iota(jnp.int32, (NRHS, 2 * RANK), 1)
    far = []
    for u in range(TIERS):
        span = 1 << u
        live = count[0, u]
        sums = []
        for s in range(SLOTS):
            block = got[pl.ds(partner[0, s, u] * span, span)].astype(F32)
            total = jnp.where(s < live, jnp.sum(block, axis=0), 0.0)
            sums.append(total if s % 2 == u % 2 else pltpu.roll(total, RANK, 1))
        chosen = jnp.concatenate(
            [
                jnp.where(lane < RANK, sums[0], sums[1]),
                jnp.where(lane < RANK, sums[2], sums[3]),
            ],
            axis=1,
        )
        rows = slice(u * 256, (u + 1) * 256)
        far.append(folded(stacked(chosen), pairs[0, rows], pairs[1, rows]))
    down = far[TIERS - 1]
    for u in reversed(range(TIERS - 1)):
        at = TIERS * 256 + u * RANK
        rows = slice(at, at + RANK)
        down = far[u] + folded(stacked(down), pairs[0, rows], pairs[1, rows])
    leaf_field = field[...] + folded(stacked(down), paths[0], paths[1])
    both = stacked(leaf_field)
    for l in range(LEAVES):
        total = mxu(both[:, l * RANK : (l + 1) * RANK], row_basis[l])
        if 2 <= l < LEAVES - 2:
            near = near_inner[:, (l - 2) * LEAF_LEN : (l - 1) * LEAF_LEN]
        else:
            i = l if l < 2 else l - (LEAVES - 4)
            near = near_edge[:, i * LEAF_LEN : (i + 1) * LEAF_LEN]
        out[:, l * LEAF_LEN : (l + 1) * LEAF_LEN] = near + total[:NRHS] + total[NRHS:]


VMEM = pl.BlockSpec(memory_space=pltpu.VMEM)
SMEM = pl.BlockSpec(memory_space=pltpu.SMEM)
HBM = pl.BlockSpec(memory_space=pltpu.HBM)


def held(shape, dtype):
    return pltpu.VMEM(shape, dtype)


def far_away(value):
    return pltpu.with_memory_space_constraint(value, pltpu.HBM)


LIMIT = pltpu.CompilerParams(vmem_limit_bytes=32 * 1024 * 1024)


def cost(flops, size):
    return pl.CostEstimate(flops=flops, bytes_accessed=size, transcendentals=0)


def body(
    rhs,
    col_basis,
    row_basis,
    near_blocks,
    near_partner,
    near_count,
    col_transfer_local,
    row_transfer_local,
    local_coupling,
    local_partner,
    local_count,
    col_transfer_up,
    row_transfer_up,
    up_coupling,
    up_partner,
    up_count,
):
    shape = jax.ShapeDtypeStruct
    blocks, coeffs, halo_first, halo_second, rhs_held, near_held = pl.pallas_call(
        up_kernel,
        out_shape=(
            shape((NDEV, NRHS, 2 * RANK), BF16),
            held((28, NRHS, RANK), F32),
            held((NRHS, HALO), BF16),
            held((NRHS, HALO), BF16),
            held(rhs.shape, BF16),
            held((EARLY,) + near_blocks.shape[1:], BF16),
        ),
        in_specs=[HBM] * 5,
        out_specs=(VMEM,) * 6,
        scratch_shapes=[
            pltpu.VMEM(col_basis.shape, BF16),
            pltpu.VMEM(col_transfer_local.shape, F32),
            pltpu.VMEM(col_transfer_up.shape, F32),
            pltpu.SemaphoreType.DMA((5,)),
            pltpu.VMEM((NRHS, HALO), BF16),
            pltpu.VMEM((NRHS, HALO), BF16),
        ],
        compiler_params=LIMIT,
        cost_estimate=cost(2 * 10**7, 10**7),
    )(*map(far_away, (rhs, col_basis, col_transfer_local, col_transfer_up, near_blocks)))
    firsts = [(i, i ^ 1) for i in range(NDEV)]
    seconds = [(i, ((i + 1) ^ 1) - 1) for i in range(1, NDEV - 1)]
    got = lax.all_to_all(blocks, AXES, 0, 0)
    first = lax.ppermute(halo_first, AXES, firsts)
    second = lax.ppermute(halo_second, AXES, seconds)
    partner = near_partner.T
    near_inner, paths, coupling_held, local_held = pl.pallas_call(
        inner_kernel,
        out_shape=(
            held((NRHS, (LEAVES - 4) * LEAF_LEN), F32),
            held((2, RANK, LEAVES * RANK), BF16),
            held((12,) + local_coupling.shape[1:], F32),
            held(row_transfer_local.shape, F32),
        ),
        in_specs=[VMEM, VMEM, HBM, SMEM, SMEM, HBM, HBM],
        out_specs=(VMEM,) * 4,
        scratch_shapes=[
            pltpu.VMEM((LEAVES - 4 - EARLY,) + near_blocks.shape[1:], BF16),
            pltpu.SemaphoreType.DMA((LEAVES - 2 - EARLY,)),
        ],
        compiler_params=LIMIT,
        cost_estimate=cost(2 * 10**8, 10**7),
    )(
        rhs_held,
        near_held,
        far_away(near_blocks),
        partner,
        near_count,
        far_away(local_coupling),
        far_away(row_transfer_local),
    )
    entries = 28 + 3 * (ZERO + 1)
    near_edge, field, pairs, basis_held = pl.pallas_call(
        edge_kernel,
        out_shape=(
            held((NRHS, 4 * LEAF_LEN), F32),
            held((NRHS, LEAVES * RANK), F32),
            held((2, TIERS * 256 + (TIERS - 1) * RANK, RANK), BF16),
            held(row_basis.shape, BF16),
        ),
        in_specs=[VMEM] * 4 + [HBM, SMEM, SMEM, HBM, VMEM, SMEM, SMEM, VMEM] + [HBM] * 3,
        out_specs=(VMEM,) * 4,
        scratch_shapes=[
            pltpu.VMEM((LEAVES,) + local_coupling.shape[1:], F32),
            pltpu.VMEM(row_transfer_up.shape, F32),
            pltpu.VMEM(up_coupling.shape, F32),
            pltpu.VMEM((4,) + near_blocks.shape[1:], BF16),
            pltpu.SemaphoreType.DMA((8,)),
            pltpu.VMEM((NRHS, LEAVES * LEAF_LEN + 2 * EDGE), BF16),
            pltpu.VMEM((entries, 2 * NRHS, 2 * RANK), F32),
            pltpu.VMEM((entries, 2 * NRHS, 2 * RANK), F32),
        ],
        compiler_params=LIMIT,
        cost_estimate=cost(10**8, 5 * 10**6),
    )(
        rhs_held,
        first,
        second,
        coeffs,
        far_away(near_blocks),
        partner,
        near_count,
        far_away(local_coupling),
        coupling_held,
        local_partner.T,
        local_count,
        local_held,
        *map(far_away, (row_transfer_up, up_coupling, row_basis)),
    )
    return pl.pallas_call(
        final_kernel,
        out_shape=shape((NRHS, LEAVES * LEAF_LEN), F32),
        in_specs=[VMEM, SMEM, SMEM] + [VMEM] * 6,
        out_specs=VMEM,
        compiler_params=LIMIT,
        cost_estimate=cost(2 * 10**7, 3 * 10**6),
    )(
        got,
        up_partner.transpose(0, 2, 1),
        up_count,
        pairs,
        paths,
        field,
        near_inner,
        near_edge,
        basis_held,
    )


def solution(mesh):
    return jax.shard_map(
        body,
        mesh=mesh,
        in_specs=(
            P(None, AXES),
            P(AXES, None, None),
            P(AXES, None, None),
            P(AXES, None, None, None),
            P(AXES, None),
            P(AXES),
            P(AXES, None, None),
            P(AXES, None, None),
            P(AXES, None, None, None),
            P(AXES, None),
            P(AXES),
            P(AXES, None, None, None),
            P(AXES, None, None, None),
            P(AXES, None, None, None, None),
            P(AXES, None, None),
            P(AXES, None),
        ),
        out_specs=P(None, AXES),
        check_vma=False,
    )
```

```python
import jax
import jax.numpy as jnp
from jax import lax
from jax.experimental import pallas as pl
from jax.experimental.pallas import tpu as pltpu
from jax.sharding import PartitionSpec as P

AXES = ("leaf", "slab")
F32 = jnp.float32
BF16 = jnp.bfloat16
LEAVES = 16
LEAF_LEN = 256
RANK = 64
NRHS = 8
TIERS = 7
SLOTS = 4
NDEV = 256
BOXES = (8, 4, 4, 2)
STARTS = (0, 16, 24, 28)
ROWS = (0, 16, 24)
EDGE = 2 * LEAF_LEN
HALO = EDGE + 10 * RANK
ZERO = 6
EARLY = 6


def mxu(left, right):
    return lax.dot_general(left, right, (((1,), (0,)), ((), ())), preferred_element_type=F32)


def mxu_t(left, right):
    return lax.dot_general(left, right, (((1,), (1,)), ((), ())), preferred_element_type=F32)


def split(value):
    high = value.astype(BF16)
    return high, (value - high.astype(F32)).astype(BF16)


def stacked(value):
    high = value.astype(BF16).astype(F32)
    return jnp.concatenate([high, value - high], axis=0).astype(BF16)


def folded(left, high, low):
    total = mxu(left, high) + mxu(left, low)
    half = total.shape[0] // 2
    return total[:half] + total[half:]


def product(left, right):
    return folded(stacked(left), *split(right))


def fetch(sources, targets, sems):
    copies = [
        pltpu.make_async_copy(source, target, sems.at[i])
        for i, (source, target) in enumerate(zip(sources, targets))
    ]
    for copy in copies:
        copy.start()
    return copies


def box(tier, cluster):
    first = cluster * (1 << tier)
    z = lax.shift_right_logical(first, 3) & 7
    y = lax.shift_right_logical(first, 6)
    x = first & 3
    core = lax.shift_right_logical(first, 2) & 1
    return (
        pl.ds(z, 1 << max(tier - 3, 0)),
        pl.ds(y, 1),
        pl.ds(x, 1 << min(tier, 2)),
        pl.ds(core, 2 if tier > 2 else 1),
    )


def exchange_order():
    return [
        ((y * 8 + z) * 2 + core) * 4 + x
        for z in range(8)
        for y in range(4)
        for x in range(4)
        for core in range(2)
    ]


def up_kernel(
    rhs_in,
    basis_in,
    local_in,
    up_in,
    near_in,
    blocks,
    coeffs,
    halo_first,
    halo_second,
    rhs,
    near_blocks,
    col_basis,
    col_local,
    col_up,
    sems,
    halo_up,
    halo_down,
):
    me = lax.axis_index("leaf") * 4 + lax.axis_index("slab")
    copies = fetch(
        (rhs_in, basis_in, local_in, up_in, near_in.at[pl.ds(2, EARLY)]),
        (rhs, col_basis, col_local, col_up, near_blocks),
        sems,
    )
    blocks[...] = jnp.zeros_like(blocks)
    copies[0].wait()
    copies[1].wait()
    level = [
        mxu_t(rhs[:, l * LEAF_LEN : (l + 1) * LEAF_LEN], col_basis[l]) for l in range(LEAVES)
    ]
    copies[2].wait()
    for h in range(4):
        width = LEAVES >> h
        if h < 3:
            for c in range(width):
                coeffs[ROWS[h] + c] = level[c]
            for i in range(3):
                at = EDGE + (h * 3 + i) * RANK
                halo_up[:, at : at + RANK] = level[width - 3 + i].astype(BF16)
                halo_down[:, at : at + RANK] = level[i].astype(BF16)
        above = []
        for j in range(width // 2):
            pair = jnp.concatenate([level[2 * j], level[2 * j + 1]], axis=1)
            moves = col_local[STARTS[h] + 2 * j : STARTS[h] + 2 * j + 2].reshape(2 * RANK, RANK)
            above.append(product(pair, moves))
        level = above
    halo_up[:, :EDGE] = rhs[:, (LEAVES - 2) * LEAF_LEN :]
    halo_down[:, :EDGE] = rhs[:, :EDGE]
    halo_up[:, HALO - RANK :] = jnp.zeros((NRHS, RANK), BF16)
    halo_down[:, HALO - RANK :] = jnp.zeros((NRHS, RANK), BF16)
    even = me % 2 == 0
    halo_first[...] = jnp.where(even, halo_up[...], halo_down[...])
    halo_second[...] = jnp.where(even, halo_down[...], halo_up[...])
    copies[3].wait()
    share = level[0]
    sent = [share.astype(BF16)]
    for u in range(TIERS - 1):
        share = product(share, col_up[0, u])
        sent.append(share.astype(BF16))
    for u in reversed(range(TIERS)):
        side = (u % 2) * RANK
        own = lax.shift_right_logical(me, u)
        for off in (-3, -2, 2, 3):
            there = own + off
            there = jnp.where((there >= 0) & (there < (NDEV >> u)), there, own)
            place = box(u, there)
            sizes = tuple(part.size for part in place)
            blocks[(*place, slice(None), slice(side, side + RANK))] = jnp.broadcast_to(
                sent[u], sizes + (NRHS, RANK)
            )
    copies[4].wait()


def near_leaf(l, me, window, shift, blocks, partner, count):
    total = None
    for s in range(3):
        spot = partner[s, l] - me * LEAVES + shift
        part = window[:, pl.ds(pl.multiple_of(spot * LEAF_LEN, LEAF_LEN), LEAF_LEN)]
        if s == 2:
            part = jnp.where(count[l] > s, part, jnp.zeros_like(part))
        term = mxu_t(part, blocks[s])
        total = term if total is None else total + term
    return total


def inner_kernel(
    rhs,
    near_early,
    near_in,
    partner,
    count,
    coupling_in,
    local_in,
    near,
    paths,
    coupling,
    row_local,
    near_blocks,
    sems,
):
    me = lax.axis_index("leaf") * 4 + lax.axis_index("slab")
    late = LEAVES - 4 - EARLY
    copies = fetch(
        [local_in, coupling_in.at[pl.ds(LEAVES, 12)]]
        + [near_in.at[2 + EARLY + i] for i in range(late)],
        [row_local, coupling] + [near_blocks.at[i] for i in range(late)],
        sems,
    )
    for l in range(2, LEAVES - 2):
        i = l - 2 - EARLY
        if i >= 0:
            copies[2 + i].wait()
        near[:, (l - 2) * LEAF_LEN : (l - 1) * LEAF_LEN] = near_leaf(
            l, me, rhs, 0, near_early.at[l - 2] if i < 0 else near_blocks.at[i], partner, count
        )
    copies[0].wait()
    level = [row_local[STARTS[3] + c] for c in range(2)]
    for h in (2, 1, 0):
        level = [
            product(level[c // 2], row_local[STARTS[h] + c]) for c in range(LEAVES >> h)
        ]
    for l in range(LEAVES):
        high, low = split(level[l])
        paths[0, :, l * RANK : (l + 1) * RANK] = high
        paths[1, :, l * RANK : (l + 1) * RANK] = low
    copies[1].wait()


def edge_kernel(
    rhs,
    first,
    second,
    coeffs,
    near_in,
    partner,
    count,
    coupling_in,
    coupling_held,
    local_partner,
    local_count,
    row_local,
    up_in,
    pairs_in,
    basis_in,
    near,
    field,
    pairs,
    row_basis,
    coupling,
    row_up,
    up_coupling,
    near_blocks,
    sems,
    window,
    left,
    right,
):
    me = lax.axis_index("leaf") * 4 + lax.axis_index("slab")
    edges = (0, 1, LEAVES - 2, LEAVES - 1)
    copies = fetch(
        [coupling_in.at[pl.ds(0, LEAVES)]]
        + [near_in.at[l] for l in edges]
        + [pairs_in, up_in, basis_in],
        [coupling]
        + [near_blocks.at[i] for i in range(4)]
        + [up_coupling, row_up, row_basis],
        sems,
    )
    even = me % 2 == 0
    from_low = jnp.where(even, second[...], first[...])
    from_high = jnp.where(even, first[...], second[...])
    window[:, :EDGE] = from_low[:, :EDGE]
    window[:, EDGE : EDGE + LEAVES * LEAF_LEN] = rhs[...]
    window[:, EDGE + LEAVES * LEAF_LEN :] = from_high[:, :EDGE]
    blank = jnp.zeros((2 * NRHS, RANK), F32)

    def place(at, value):
        high = value.astype(BF16).astype(F32)
        both = jnp.concatenate([high, value - high], axis=0)
        left[at] = jnp.concatenate([both, blank], axis=1)
        right[at] = jnp.concatenate([blank, both], axis=1)

    bases = []
    base = 0
    for h in range(3):
        width = LEAVES >> h
        for i in range(3):
            at = EDGE + (h * 3 + i) * RANK
            place(base + i, from_low[:, at : at + RANK].astype(F32))
            place(base + 3 + width + i, from_high[:, at : at + RANK].astype(F32))
        for c in range(width):
            place(base + 3 + c, coeffs[ROWS[h] + c])
        left[base + width + ZERO] = jnp.zeros((2 * NRHS, 2 * RANK), F32)
        right[base + width + ZERO] = jnp.zeros((2 * NRHS, 2 * RANK), F32)
        bases.append(base)
        base += width + ZERO + 1

    def couple(h, c, matrices):
        row = ROWS[h] + c
        live = local_count[row]
        start = bases[h] + 3 - me * (LEAVES >> h)
        none = bases[h] + (LEAVES >> h) + ZERO
        spots = [
            jnp.where(s < live, local_partner[s, row] + start, none) for s in range(SLOTS)
        ]
        chosen = jnp.concatenate(
            [left[spots[0]] + right[spots[1]], left[spots[2]] + right[spots[3]]], axis=1
        ).astype(BF16)
        return folded(chosen, *split(matrices.reshape(SLOTS * RANK, RANK)))

    level = [couple(2, c, coupling_held[8 + c]) for c in range(4)]
    level = [
        couple(1, c, coupling_held[c]) + product(level[c // 2], row_local[STARTS[1] + c])
        for c in range(8)
    ]
    level = [product(level[c // 2], row_local[c]) for c in range(LEAVES)]
    copies[0].wait()
    for l in range(LEAVES):
        field[:, l * RANK : (l + 1) * RANK] = level[l] + couple(0, l, coupling[l])
    for i, l in enumerate(edges):
        copies[1 + i].wait()
        near[:, i * LEAF_LEN : (i + 1) * LEAF_LEN] = near_leaf(
            l, me, window, 2, near_blocks.at[i], partner, count
        )
    copies[5].wait()
    copies[6].wait()
    for u in range(TIERS):
        high, low = split(up_coupling[0, u].reshape(SLOTS * RANK, RANK))
        pairs[0, u * 256 : (u + 1) * 256] = high
        pairs[1, u * 256 : (u + 1) * 256] = low
    for u in range(TIERS - 1):
        high, low = split(row_up[0, u])
        at = TIERS * 256 + u * RANK
        pairs[0, at : at + RANK] = high
        pairs[1, at : at + RANK] = low
    copies[7].wait()


def final_kernel(
    got, partner, count, pairs, paths, field, near_inner, near_edge, row_basis, out
):
    lane = lax.broadcasted_iota(jnp.int32, (NRHS, 2 * RANK), 1)
    far = []
    for u in range(TIERS):
        live = count[0, u]
        sums = []
        for s in range(SLOTS):
            block = got[box(u, partner[0, s, u])].astype(F32)
            total = jnp.sum(block.reshape(1 << u, NRHS, 2 * RANK), axis=0)
            total = jnp.where(s < live, total, 0.0)
            sums.append(total if s % 2 == u % 2 else pltpu.roll(total, RANK, 1))
        chosen = jnp.concatenate(
            [
                jnp.where(lane < RANK, sums[0], sums[1]),
                jnp.where(lane < RANK, sums[2], sums[3]),
            ],
            axis=1,
        )
        rows = slice(u * 256, (u + 1) * 256)
        far.append(folded(stacked(chosen), pairs[0, rows], pairs[1, rows]))
    down = far[TIERS - 1]
    for u in reversed(range(TIERS - 1)):
        at = TIERS * 256 + u * RANK
        rows = slice(at, at + RANK)
        down = far[u] + folded(stacked(down), pairs[0, rows], pairs[1, rows])
    leaf_field = field[...] + folded(stacked(down), paths[0], paths[1])
    both = stacked(leaf_field)
    for l in range(LEAVES):
        total = mxu(both[:, l * RANK : (l + 1) * RANK], row_basis[l])
        if 2 <= l < LEAVES - 2:
            near = near_inner[:, (l - 2) * LEAF_LEN : (l - 1) * LEAF_LEN]
        else:
            i = l if l < 2 else l - (LEAVES - 4)
            near = near_edge[:, i * LEAF_LEN : (i + 1) * LEAF_LEN]
        out[:, l * LEAF_LEN : (l + 1) * LEAF_LEN] = near + total[:NRHS] + total[NRHS:]


VMEM = pl.BlockSpec(memory_space=pltpu.VMEM)
SMEM = pl.BlockSpec(memory_space=pltpu.SMEM)
HBM = pl.BlockSpec(memory_space=pltpu.HBM)


def held(shape, dtype):
    return pltpu.VMEM(shape, dtype)


def far_away(value):
    return pltpu.with_memory_space_constraint(value, pltpu.HBM)


LIMIT = pltpu.CompilerParams(vmem_limit_bytes=32 * 1024 * 1024)


def cost(flops, size):
    return pl.CostEstimate(flops=flops, bytes_accessed=size, transcendentals=0)


def body(
    rhs,
    col_basis,
    row_basis,
    near_blocks,
    near_partner,
    near_count,
    col_transfer_local,
    row_transfer_local,
    local_coupling,
    local_partner,
    local_count,
    col_transfer_up,
    row_transfer_up,
    up_coupling,
    up_partner,
    up_count,
):
    shape = jax.ShapeDtypeStruct
    blocks, coeffs, halo_first, halo_second, rhs_held, near_held = pl.pallas_call(
        up_kernel,
        out_shape=(
            shape(BOXES + (NRHS, 2 * RANK), BF16),
            held((28, NRHS, RANK), F32),
            held((NRHS, HALO), BF16),
            held((NRHS, HALO), BF16),
            held(rhs.shape, BF16),
            held((EARLY,) + near_blocks.shape[1:], BF16),
        ),
        in_specs=[HBM] * 5,
        out_specs=(VMEM,) * 6,
        scratch_shapes=[
            pltpu.VMEM(col_basis.shape, BF16),
            pltpu.VMEM(col_transfer_local.shape, F32),
            pltpu.VMEM(col_transfer_up.shape, F32),
            pltpu.SemaphoreType.DMA((5,)),
            pltpu.VMEM((NRHS, HALO), BF16),
            pltpu.VMEM((NRHS, HALO), BF16),
        ],
        compiler_params=LIMIT,
        cost_estimate=cost(2 * 10**7, 10**7),
    )(*map(far_away, (rhs, col_basis, col_transfer_local, col_transfer_up, near_blocks)))
    firsts = [(i, i ^ 1) for i in range(NDEV)]
    seconds = [(i, ((i + 1) ^ 1) - 1) for i in range(1, NDEV - 1)]
    got = lax.all_to_all(
        blocks.reshape(NDEV, NRHS, 2 * RANK),
        AXES,
        0,
        0,
        axis_index_groups=[exchange_order()],
    ).reshape(BOXES + (NRHS, 2 * RANK))
    first = lax.ppermute(halo_first, AXES, firsts)
    second = lax.ppermute(halo_second, AXES, seconds)
    partner = near_partner.T
    near_inner, paths, coupling_held, local_held = pl.pallas_call(
        inner_kernel,
        out_shape=(
            held((NRHS, (LEAVES - 4) * LEAF_LEN), F32),
            held((2, RANK, LEAVES * RANK), BF16),
            held((12,) + local_coupling.shape[1:], F32),
            held(row_transfer_local.shape, F32),
        ),
        in_specs=[VMEM, VMEM, HBM, SMEM, SMEM, HBM, HBM],
        out_specs=(VMEM,) * 4,
        scratch_shapes=[
            pltpu.VMEM((LEAVES - 4 - EARLY,) + near_blocks.shape[1:], BF16),
            pltpu.SemaphoreType.DMA((LEAVES - 2 - EARLY,)),
        ],
        compiler_params=LIMIT,
        cost_estimate=cost(2 * 10**8, 10**7),
    )(
        rhs_held,
        near_held,
        far_away(near_blocks),
        partner,
        near_count,
        far_away(local_coupling),
        far_away(row_transfer_local),
    )
    entries = 28 + 3 * (ZERO + 1)
    near_edge, field, pairs, basis_held = pl.pallas_call(
        edge_kernel,
        out_shape=(
            held((NRHS, 4 * LEAF_LEN), F32),
            held((NRHS, LEAVES * RANK), F32),
            held((2, TIERS * 256 + (TIERS - 1) * RANK, RANK), BF16),
            held(row_basis.shape, BF16),
        ),
        in_specs=[VMEM] * 4 + [HBM, SMEM, SMEM, HBM, VMEM, SMEM, SMEM, VMEM] + [HBM] * 3,
        out_specs=(VMEM,) * 4,
        scratch_shapes=[
            pltpu.VMEM((LEAVES,) + local_coupling.shape[1:], F32),
            pltpu.VMEM(row_transfer_up.shape, F32),
            pltpu.VMEM(up_coupling.shape, F32),
            pltpu.VMEM((4,) + near_blocks.shape[1:], BF16),
            pltpu.SemaphoreType.DMA((8,)),
            pltpu.VMEM((NRHS, LEAVES * LEAF_LEN + 2 * EDGE), BF16),
            pltpu.VMEM((entries, 2 * NRHS, 2 * RANK), F32),
            pltpu.VMEM((entries, 2 * NRHS, 2 * RANK), F32),
        ],
        compiler_params=LIMIT,
        cost_estimate=cost(10**8, 5 * 10**6),
    )(
        rhs_held,
        first,
        second,
        coeffs,
        far_away(near_blocks),
        partner,
        near_count,
        far_away(local_coupling),
        coupling_held,
        local_partner.T,
        local_count,
        local_held,
        *map(far_away, (row_transfer_up, up_coupling, row_basis)),
    )
    return pl.pallas_call(
        final_kernel,
        out_shape=shape((NRHS, LEAVES * LEAF_LEN), F32),
        in_specs=[VMEM, SMEM, SMEM] + [VMEM] * 6,
        out_specs=VMEM,
        compiler_params=LIMIT,
        cost_estimate=cost(2 * 10**7, 3 * 10**6),
    )(
        got,
        up_partner.transpose(0, 2, 1),
        up_count,
        pairs,
        paths,
        field,
        near_inner,
        near_edge,
        basis_held,
    )


def solution(mesh):
    return jax.shard_map(
        body,
        mesh=mesh,
        in_specs=(
            P(None, AXES),
            P(AXES, None, None),
            P(AXES, None, None),
            P(AXES, None, None, None),
            P(AXES, None),
            P(AXES),
            P(AXES, None, None),
            P(AXES, None, None),
            P(AXES, None, None, None),
            P(AXES, None),
            P(AXES),
            P(AXES, None, None, None),
            P(AXES, None, None, None),
            P(AXES, None, None, None, None),
            P(AXES, None, None),
            P(AXES, None),
        ),
        out_specs=P(None, AXES),
        check_vma=False,
    )
```

```python
import jax
import jax.numpy as jnp
from jax import lax
from jax.experimental import pallas as pl
from jax.experimental.pallas import tpu as pltpu
from jax.sharding import PartitionSpec as P

AXES = ("leaf", "slab")
F32 = jnp.float32
BF16 = jnp.bfloat16
LEAVES = 16
LEAF_LEN = 256
RANK = 64
NRHS = 8
TIERS = 7
SLOTS = 4
NDEV = 256
BOXES = (8, 4, 4, 2)
STARTS = (0, 16, 24, 28)
ROWS = (0, 16, 24)
EDGE = 2 * LEAF_LEN
HALO = EDGE + 10 * RANK
ZERO = 6
EARLY = 6
PIECE = 4


def mxu(left, right):
    return lax.dot_general(left, right, (((1,), (0,)), ((), ())), preferred_element_type=F32)


def mxu_t(left, right):
    return lax.dot_general(left, right, (((1,), (1,)), ((), ())), preferred_element_type=F32)


def split(value):
    high = value.astype(BF16)
    return high, (value - high.astype(F32)).astype(BF16)


def stacked(value):
    high = value.astype(BF16).astype(F32)
    return jnp.concatenate([high, value - high], axis=0).astype(BF16)


def folded(left, high, low):
    total = mxu(left, high) + mxu(left, low)
    half = total.shape[0] // 2
    return total[:half] + total[half:]


def product(left, right):
    return folded(stacked(left), *split(right))


def fetch(sources, targets, sems):
    copies = [
        pltpu.make_async_copy(source, target, sems.at[i])
        for i, (source, target) in enumerate(zip(sources, targets))
    ]
    for copy in copies:
        copy.start()
    return copies


def box(tier, cluster):
    first = cluster * (1 << tier)
    z = lax.shift_right_logical(first, 3) & 7
    y = lax.shift_right_logical(first, 6)
    x = first & 3
    core = lax.shift_right_logical(first, 2) & 1
    return (
        pl.ds(z, 1 << max(tier - 3, 0)),
        pl.ds(y, 1),
        pl.ds(x, 1 << min(tier, 2)),
        pl.ds(core, 2 if tier > 2 else 1),
    )


def exchange_order():
    return [
        ((y * 8 + z) * 2 + core) * 4 + x
        for z in range(8)
        for y in range(4)
        for x in range(4)
        for core in range(2)
    ]


def up_kernel(
    rhs_in,
    basis_in,
    local_in,
    up_in,
    near_in,
    blocks,
    coeffs,
    halo_first,
    halo_second,
    rhs,
    near_blocks,
    col_basis,
    col_local,
    col_up,
    sems,
    halo_up,
    halo_down,
):
    me = lax.axis_index("leaf") * 4 + lax.axis_index("slab")
    copies = fetch(
        (rhs_in, basis_in, local_in, up_in, near_in.at[pl.ds(2, EARLY)]),
        (rhs, col_basis, col_local, col_up, near_blocks),
        sems,
    )
    blocks[...] = jnp.zeros_like(blocks)
    copies[0].wait()
    copies[1].wait()
    level = [
        mxu_t(rhs[:, l * LEAF_LEN : (l + 1) * LEAF_LEN], col_basis[l]) for l in range(LEAVES)
    ]
    copies[2].wait()
    for h in range(4):
        width = LEAVES >> h
        if h < 3:
            for c in range(width):
                coeffs[ROWS[h] + c] = level[c]
            for i in range(3):
                at = EDGE + (h * 3 + i) * RANK
                halo_up[:, at : at + RANK] = level[width - 3 + i].astype(BF16)
                halo_down[:, at : at + RANK] = level[i].astype(BF16)
        above = []
        for j in range(width // 2):
            pair = jnp.concatenate([level[2 * j], level[2 * j + 1]], axis=1)
            moves = col_local[STARTS[h] + 2 * j : STARTS[h] + 2 * j + 2].reshape(2 * RANK, RANK)
            above.append(product(pair, moves))
        level = above
    halo_up[:, :EDGE] = rhs[:, (LEAVES - 2) * LEAF_LEN :]
    halo_down[:, :EDGE] = rhs[:, :EDGE]
    halo_up[:, HALO - RANK :] = jnp.zeros((NRHS, RANK), BF16)
    halo_down[:, HALO - RANK :] = jnp.zeros((NRHS, RANK), BF16)
    even = me % 2 == 0
    halo_first[...] = jnp.where(even, halo_up[...], halo_down[...])
    halo_second[...] = jnp.where(even, halo_down[...], halo_up[...])
    copies[3].wait()
    share = level[0]
    sent = [share.astype(BF16)]
    for u in range(TIERS - 1):
        share = product(share, col_up[0, u])
        sent.append(share.astype(BF16))
    for u in reversed(range(TIERS)):
        side = (u % 2) * RANK
        own = lax.shift_right_logical(me, u)
        for off in (-3, -2, 2, 3):
            there = own + off
            there = jnp.where((there >= 0) & (there < (NDEV >> u)), there, own)
            place = box(u, there)
            sizes = tuple(part.size for part in place)
            blocks[(*place, slice(None), slice(side, side + RANK))] = jnp.broadcast_to(
                sent[u], sizes + (NRHS, RANK)
            )
    copies[4].wait()


def near_leaf(l, me, window, shift, blocks, partner, count):
    total = None
    for s in range(3):
        spot = partner[s, l] - me * LEAVES + shift
        part = window[:, pl.ds(pl.multiple_of(spot * LEAF_LEN, LEAF_LEN), LEAF_LEN)]
        if s == 2:
            part = jnp.where(count[l] > s, part, jnp.zeros_like(part))
        term = mxu_t(part, blocks[s])
        total = term if total is None else total + term
    return total


def inner_kernel(
    rhs,
    near_early,
    near_in,
    partner,
    count,
    coupling_in,
    local_in,
    near,
    paths,
    coupling,
    row_local,
    near_blocks,
    sems,
):
    me = lax.axis_index("leaf") * 4 + lax.axis_index("slab")
    late = LEAVES - 4 - EARLY
    copies = fetch(
        [local_in, coupling_in.at[pl.ds(LEAVES, 12)]]
        + [near_in.at[2 + EARLY + i] for i in range(late)],
        [row_local, coupling] + [near_blocks.at[i] for i in range(late)],
        sems,
    )
    for l in range(2, LEAVES - 2):
        i = l - 2 - EARLY
        if i >= 0:
            copies[2 + i].wait()
        near[:, (l - 2) * LEAF_LEN : (l - 1) * LEAF_LEN] = near_leaf(
            l, me, rhs, 0, near_early.at[l - 2] if i < 0 else near_blocks.at[i], partner, count
        )
    copies[0].wait()
    level = [row_local[STARTS[3] + c] for c in range(2)]
    for h in (2, 1, 0):
        level = [
            product(level[c // 2], row_local[STARTS[h] + c]) for c in range(LEAVES >> h)
        ]
    for l in range(LEAVES):
        high, low = split(level[l])
        paths[0, :, l * RANK : (l + 1) * RANK] = high
        paths[1, :, l * RANK : (l + 1) * RANK] = low
    copies[1].wait()


def edge_kernel(
    rhs,
    first,
    second,
    coeffs,
    near_in,
    partner,
    count,
    coupling_in,
    coupling_held,
    local_partner,
    local_count,
    row_local,
    up_in,
    pairs_in,
    basis_in,
    near,
    field,
    pairs,
    row_basis,
    coupling,
    row_up,
    up_coupling,
    near_blocks,
    sems,
    window,
    left,
    right,
):
    me = lax.axis_index("leaf") * 4 + lax.axis_index("slab")
    edges = (0, 1, LEAVES - 2, LEAVES - 1)
    copies = fetch(
        [coupling_in.at[pl.ds(0, LEAVES)]]
        + [near_in.at[l] for l in edges]
        + [pairs_in, up_in, basis_in],
        [coupling]
        + [near_blocks.at[i] for i in range(4)]
        + [up_coupling, row_up, row_basis],
        sems,
    )
    even = me % 2 == 0
    from_low = jnp.where(even, second[...], first[...])
    from_high = jnp.where(even, first[...], second[...])
    window[:, :EDGE] = from_low[:, :EDGE]
    window[:, EDGE : EDGE + LEAVES * LEAF_LEN] = rhs[...]
    window[:, EDGE + LEAVES * LEAF_LEN :] = from_high[:, :EDGE]
    blank = jnp.zeros((2 * NRHS, RANK), F32)

    def place(at, value):
        high = value.astype(BF16).astype(F32)
        both = jnp.concatenate([high, value - high], axis=0)
        left[at] = jnp.concatenate([both, blank], axis=1)
        right[at] = jnp.concatenate([blank, both], axis=1)

    bases = []
    base = 0
    for h in range(3):
        width = LEAVES >> h
        for i in range(3):
            at = EDGE + (h * 3 + i) * RANK
            place(base + i, from_low[:, at : at + RANK].astype(F32))
            place(base + 3 + width + i, from_high[:, at : at + RANK].astype(F32))
        for c in range(width):
            place(base + 3 + c, coeffs[ROWS[h] + c])
        left[base + width + ZERO] = jnp.zeros((2 * NRHS, 2 * RANK), F32)
        right[base + width + ZERO] = jnp.zeros((2 * NRHS, 2 * RANK), F32)
        bases.append(base)
        base += width + ZERO + 1

    def couple(h, c, matrices):
        row = ROWS[h] + c
        live = local_count[row]
        start = bases[h] + 3 - me * (LEAVES >> h)
        none = bases[h] + (LEAVES >> h) + ZERO
        spots = [
            jnp.where(s < live, local_partner[s, row] + start, none) for s in range(SLOTS)
        ]
        chosen = jnp.concatenate(
            [left[spots[0]] + right[spots[1]], left[spots[2]] + right[spots[3]]], axis=1
        ).astype(BF16)
        return folded(chosen, *split(matrices.reshape(SLOTS * RANK, RANK)))

    level = [couple(2, c, coupling_held[8 + c]) for c in range(4)]
    level = [
        couple(1, c, coupling_held[c]) + product(level[c // 2], row_local[STARTS[1] + c])
        for c in range(8)
    ]
    level = [product(level[c // 2], row_local[c]) for c in range(LEAVES)]
    copies[0].wait()
    for l in range(LEAVES):
        field[:, l * RANK : (l + 1) * RANK] = level[l] + couple(0, l, coupling[l])
    for i, l in enumerate(edges):
        copies[1 + i].wait()
        near[:, i * LEAF_LEN : (i + 1) * LEAF_LEN] = near_leaf(
            l, me, window, 2, near_blocks.at[i], partner, count
        )
    copies[5].wait()
    copies[6].wait()
    for u in range(TIERS):
        high, low = split(up_coupling[0, u].reshape(SLOTS * RANK, RANK))
        pairs[0, u * 256 : (u + 1) * 256] = high
        pairs[1, u * 256 : (u + 1) * 256] = low
    for u in range(TIERS - 1):
        high, low = split(row_up[0, u])
        at = TIERS * 256 + u * RANK
        pairs[0, at : at + RANK] = high
        pairs[1, at : at + RANK] = low
    copies[7].wait()


def final_kernel(
    got, partner, count, pairs, paths, field, near_inner, near_edge, row_basis, out, staged, sems
):
    lane = lax.broadcasted_iota(jnp.int32, (NRHS, 2 * RANK), 1)
    far = []
    for u in range(TIERS):
        live = count[0, u]
        sums = []
        for s in range(SLOTS):
            block = got[box(u, partner[0, s, u])].astype(F32)
            total = jnp.sum(block.reshape(1 << u, NRHS, 2 * RANK), axis=0)
            total = jnp.where(s < live, total, 0.0)
            sums.append(total if s % 2 == u % 2 else pltpu.roll(total, RANK, 1))
        chosen = jnp.concatenate(
            [
                jnp.where(lane < RANK, sums[0], sums[1]),
                jnp.where(lane < RANK, sums[2], sums[3]),
            ],
            axis=1,
        )
        rows = slice(u * 256, (u + 1) * 256)
        far.append(folded(stacked(chosen), pairs[0, rows], pairs[1, rows]))
    down = far[TIERS - 1]
    for u in reversed(range(TIERS - 1)):
        at = TIERS * 256 + u * RANK
        rows = slice(at, at + RANK)
        down = far[u] + folded(stacked(down), pairs[0, rows], pairs[1, rows])
    leaf_field = field[...] + folded(stacked(down), paths[0], paths[1])
    both = stacked(leaf_field)
    copies = []
    for l in range(LEAVES):
        total = mxu(both[:, l * RANK : (l + 1) * RANK], row_basis[l])
        if 2 <= l < LEAVES - 2:
            near = near_inner[:, (l - 2) * LEAF_LEN : (l - 1) * LEAF_LEN]
        else:
            i = l if l < 2 else l - (LEAVES - 4)
            near = near_edge[:, i * LEAF_LEN : (i + 1) * LEAF_LEN]
        staged[:, l * LEAF_LEN : (l + 1) * LEAF_LEN] = near + total[:NRHS] + total[NRHS:]
        if l % PIECE == PIECE - 1:
            part = pl.ds((l + 1 - PIECE) * LEAF_LEN, PIECE * LEAF_LEN)
            copy = pltpu.make_async_copy(staged.at[:, part], out.at[:, part], sems.at[l // PIECE])
            copy.start()
            copies.append(copy)
    for copy in copies:
        copy.wait()


VMEM = pl.BlockSpec(memory_space=pltpu.VMEM)
SMEM = pl.BlockSpec(memory_space=pltpu.SMEM)
HBM = pl.BlockSpec(memory_space=pltpu.HBM)


def held(shape, dtype):
    return pltpu.VMEM(shape, dtype)


def far_away(value):
    return pltpu.with_memory_space_constraint(value, pltpu.HBM)


LIMIT = pltpu.CompilerParams(vmem_limit_bytes=32 * 1024 * 1024)


def cost(flops, size):
    return pl.CostEstimate(flops=flops, bytes_accessed=size, transcendentals=0)


def body(
    rhs,
    col_basis,
    row_basis,
    near_blocks,
    near_partner,
    near_count,
    col_transfer_local,
    row_transfer_local,
    local_coupling,
    local_partner,
    local_count,
    col_transfer_up,
    row_transfer_up,
    up_coupling,
    up_partner,
    up_count,
):
    shape = jax.ShapeDtypeStruct
    blocks, coeffs, halo_first, halo_second, rhs_held, near_held = pl.pallas_call(
        up_kernel,
        out_shape=(
            shape(BOXES + (NRHS, 2 * RANK), BF16),
            held((28, NRHS, RANK), F32),
            held((NRHS, HALO), BF16),
            held((NRHS, HALO), BF16),
            held(rhs.shape, BF16),
            held((EARLY,) + near_blocks.shape[1:], BF16),
        ),
        in_specs=[HBM] * 5,
        out_specs=(VMEM,) * 6,
        scratch_shapes=[
            pltpu.VMEM(col_basis.shape, BF16),
            pltpu.VMEM(col_transfer_local.shape, F32),
            pltpu.VMEM(col_transfer_up.shape, F32),
            pltpu.SemaphoreType.DMA((5,)),
            pltpu.VMEM((NRHS, HALO), BF16),
            pltpu.VMEM((NRHS, HALO), BF16),
        ],
        compiler_params=LIMIT,
        cost_estimate=cost(2 * 10**7, 10**7),
    )(*map(far_away, (rhs, col_basis, col_transfer_local, col_transfer_up, near_blocks)))
    firsts = [(i, i ^ 1) for i in range(NDEV)]
    seconds = [(i, ((i + 1) ^ 1) - 1) for i in range(1, NDEV - 1)]
    got = lax.all_to_all(
        blocks.reshape(NDEV, NRHS, 2 * RANK),
        AXES,
        0,
        0,
        axis_index_groups=[exchange_order()],
    ).reshape(BOXES + (NRHS, 2 * RANK))
    first = lax.ppermute(halo_first, AXES, firsts)
    second = lax.ppermute(halo_second, AXES, seconds)
    partner = near_partner.T
    near_inner, paths, coupling_held, local_held = pl.pallas_call(
        inner_kernel,
        out_shape=(
            held((NRHS, (LEAVES - 4) * LEAF_LEN), F32),
            held((2, RANK, LEAVES * RANK), BF16),
            held((12,) + local_coupling.shape[1:], F32),
            held(row_transfer_local.shape, F32),
        ),
        in_specs=[VMEM, VMEM, HBM, SMEM, SMEM, HBM, HBM],
        out_specs=(VMEM,) * 4,
        scratch_shapes=[
            pltpu.VMEM((LEAVES - 4 - EARLY,) + near_blocks.shape[1:], BF16),
            pltpu.SemaphoreType.DMA((LEAVES - 2 - EARLY,)),
        ],
        compiler_params=LIMIT,
        cost_estimate=cost(2 * 10**8, 10**7),
    )(
        rhs_held,
        near_held,
        far_away(near_blocks),
        partner,
        near_count,
        far_away(local_coupling),
        far_away(row_transfer_local),
    )
    entries = 28 + 3 * (ZERO + 1)
    near_edge, field, pairs, basis_held = pl.pallas_call(
        edge_kernel,
        out_shape=(
            held((NRHS, 4 * LEAF_LEN), F32),
            held((NRHS, LEAVES * RANK), F32),
            held((2, TIERS * 256 + (TIERS - 1) * RANK, RANK), BF16),
            held(row_basis.shape, BF16),
        ),
        in_specs=[VMEM] * 4 + [HBM, SMEM, SMEM, HBM, VMEM, SMEM, SMEM, VMEM] + [HBM] * 3,
        out_specs=(VMEM,) * 4,
        scratch_shapes=[
            pltpu.VMEM((LEAVES,) + local_coupling.shape[1:], F32),
            pltpu.VMEM(row_transfer_up.shape, F32),
            pltpu.VMEM(up_coupling.shape, F32),
            pltpu.VMEM((4,) + near_blocks.shape[1:], BF16),
            pltpu.SemaphoreType.DMA((8,)),
            pltpu.VMEM((NRHS, LEAVES * LEAF_LEN + 2 * EDGE), BF16),
            pltpu.VMEM((entries, 2 * NRHS, 2 * RANK), F32),
            pltpu.VMEM((entries, 2 * NRHS, 2 * RANK), F32),
        ],
        compiler_params=LIMIT,
        cost_estimate=cost(10**8, 5 * 10**6),
    )(
        rhs_held,
        first,
        second,
        coeffs,
        far_away(near_blocks),
        partner,
        near_count,
        far_away(local_coupling),
        coupling_held,
        local_partner.T,
        local_count,
        local_held,
        *map(far_away, (row_transfer_up, up_coupling, row_basis)),
    )
    return pl.pallas_call(
        final_kernel,
        out_shape=shape((NRHS, LEAVES * LEAF_LEN), F32),
        in_specs=[VMEM, SMEM, SMEM] + [VMEM] * 6,
        out_specs=HBM,
        scratch_shapes=[
            pltpu.VMEM((NRHS, LEAVES * LEAF_LEN), F32),
            pltpu.SemaphoreType.DMA((LEAVES // PIECE,)),
        ],
        compiler_params=LIMIT,
        cost_estimate=cost(2 * 10**7, 3 * 10**6),
    )(
        got,
        up_partner.transpose(0, 2, 1),
        up_count,
        pairs,
        paths,
        field,
        near_inner,
        near_edge,
        basis_held,
    )


def solution(mesh):
    return jax.shard_map(
        body,
        mesh=mesh,
        in_specs=(
            P(None, AXES),
            P(AXES, None, None),
            P(AXES, None, None),
            P(AXES, None, None, None),
            P(AXES, None),
            P(AXES),
            P(AXES, None, None),
            P(AXES, None, None),
            P(AXES, None, None, None),
            P(AXES, None),
            P(AXES),
            P(AXES, None, None, None),
            P(AXES, None, None, None),
            P(AXES, None, None, None, None),
            P(AXES, None, None),
            P(AXES, None),
        ),
        out_specs=P(None, AXES),
        check_vma=False,
    )
```
